256 devices in a mesh: gx: 8 (over z), gy: 8 (over y_lo, x), gz: 4 (over y_hi, core).
Axes of the slice: x: 4, y: 4 (y_hi: 2, y_lo: 2; y = y_hi * 2 + y_lo), z: 8, core: 2. Of those that a mesh axis runs over, the one named last changes fastest.
Arguments:
- saved_inputs: bfloat16 [1024, 12288], P('gx', 'gy'), may hold values from -6 to 6
- w_first: bfloat16 [12288, 24576], P('gy', ('gx', 'gz')), may hold values from -0.0546875 to 0.0546875
- w_second: bfloat16 [24576, 12288], P(('gx', 'gz'), 'gy'), may hold values from -0.0390625 to 0.0390625
- grad_output: bfloat16 [1024, 12288], P('gx', 'gy'), may hold values from -3 to 3
Outputs:
- grad_inputs: bfloat16 [1024, 12288], P('gx', 'gy')
- grad_w_first: bfloat16 [12288, 24576], P('gy', ('gx', 'gz'))
- grad_w_second: bfloat16 [24576, 12288], P(('gx', 'gz'), 'gy')
The draws below stay inside these ranges and needn't reach their ends.
All inputs are finite; a program needn't handle non-finite values.
Results may differ from the reference program's by a relative error of at most 0.0049.
Values may be sent and summed in bfloat16 or wider, within the bound.
No kernel may reach another device: no remote copies, remote signals or barrier semaphores. Data moves between devices by JAX's collectives and lax.ppermute only.
A program may use at most 128 MiB of HBM per device.

```python
import math
import jax
import jax.numpy as jnp

D = 12288
FF = 24576
TOKENS = 1024


def levels(rng, shape, shards, smallest, top_value):
    def one(position, parts):
        heights = jax.random.uniform(jax.random.fold_in(jax.random.fold_in(rng, 6), position), (parts,), jnp.float32, smallest / len(shards), top_value / len(shards))
        return jnp.repeat(jnp.exp(heights), shape[position] // parts).reshape((-1,) + (1,) * (len(shape) - position - 1))

    level = one(*shards[0])
    for cut in shards[1:]:
        level = level * one(*cut)
    return level


def noise(key, extent, scale, bound, cuts=(), kind=jnp.bfloat16):
    factor_of = levels(key, extent, cuts, -0.22, 0.18) if cuts else 1.0
    array = jax.random.normal(key, extent, jnp.float32) * scale * factor_of
    return jnp.minimum(jnp.maximum(array, -bound), bound).astype(kind)


def setup_inputs(seed: int = 0) -> dict:
    key_of = jax.random.split(jax.random.key(seed), 5)
    return {
        "saved_inputs": noise(key_of[0], (TOKENS, D), 1.0, 6.0, ((0, 8), (1, 8))),
        "w_first": noise(key_of[1], (D, FF), D ** -0.5, 0.0546875, ((0, 8), (1, 32))),
        "w_second": noise(key_of[2], (FF, D), FF ** -0.5, 0.0390625, ((0, 32), (1, 8))),
        "grad_output": noise(key_of[3], (TOKENS, D), 0.5, 3.0, ((0, 8), (1, 8))),
    }


root_coef = math.sqrt(2.0 / math.pi)
cubic_coef = 0.044715

def gelu_pair(pre):
    inner = root_coef * (pre + cubic_coef * pre * pre * pre)
    tanh_val = jnp.tanh(inner)
    value = 0.5 * pre * (1.0 + tanh_val)
    slope = 0.5 * (1.0 + tanh_val) + 0.5 * pre * (1.0 - tanh_val * tanh_val) * root_coef * (1.0 + 3.0 * cubic_coef * pre * pre)
    return (value, slope)

def reference(saved_inputs, w_first, w_second, grad_output):
    pre = jnp.dot(saved_inputs, w_first, preferred_element_type=jnp.float32)
    grad_hidden = jnp.dot(grad_output, w_second.T, preferred_element_type=jnp.float32)
    value, slope = gelu_pair(pre)
    hidden = value.astype(jnp.bfloat16)
    grad_pre = (grad_hidden * slope).astype(jnp.bfloat16)
    grad_w_second = jnp.dot(hidden.T, grad_output, preferred_element_type=jnp.float32).astype(jnp.bfloat16)
    grad_w_first = jnp.dot(saved_inputs.T, grad_pre, preferred_element_type=jnp.float32).astype(jnp.bfloat16)
    grad_inputs = jnp.dot(grad_pre, w_first.T, preferred_element_type=jnp.float32).astype(jnp.bfloat16)
    return (grad_inputs, grad_w_first, grad_w_second)
```

```python
import math

import jax
import jax.numpy as jnp
from jax import lax
from jax.sharding import Mesh, PartitionSpec as P

root_coef = math.sqrt(2.0 / math.pi)
cubic_coef = 0.044715
BF = jnp.bfloat16
F32 = jnp.float32
GY = ("ylo", "x")
GROUPS = ((0, 1, -1), (2, -2), (3, -3, 4))


def gelu_local(pre, grad_hidden):
    inner = root_coef * (pre + cubic_coef * pre * pre * pre)
    tanh_val = jnp.tanh(inner)
    value = 0.5 * pre * (1.0 + tanh_val)
    slope = 0.5 * (1.0 + tanh_val) + 0.5 * pre * (1.0 - tanh_val * tanh_val) * root_coef * (
        1.0 + 3.0 * cubic_coef * pre * pre
    )
    return (value.astype(BF), (grad_hidden * slope).astype(BF))


def shift(a, axis, size, by):
    return lax.ppermute(a, axis, [(i, (i + by) % size) for i in range(size)])


def swap(a, axis):
    return lax.ppermute(a, axis, [(0, 1), (1, 0)])


def dot(a, b, ca, cb):
    return lax.dot_general(a, b, (((ca,), (cb,)), ((), ())), preferred_element_type=F32)


def on_device(x, w1, w2, g):
    nz = lax.axis_size("z")
    core = lax.axis_index("core")
    half = x.shape[0] // 2
    ff = w1.shape[1]
    ngy = lax.axis_size("ylo") * lax.axis_size("x")

    def part(a, which):
        return lax.dynamic_slice_in_dim(a, which * half, half, 0)

    pack = jnp.stack([part(x, core), part(g, core)])
    shards = {0: (part(x, core), part(g, core), part(x, 1 - core), part(g, 1 - core))}
    up = down = pack
    for k in range(1, nz // 2):
        up, down = shift(up, "z", nz, 1), shift(down, "z", nz, -1)
        for d, mine in ((k, up), (-k, down)):
            other = swap(mine, "core")
            shards[d] = (mine[0], mine[1], other[0], other[1])
    xs, gs = shift(up[0], "z", nz, 1), shift(down[1], "z", nz, -1)
    shards[nz // 2] = (xs, gs, swap(xs, "core"), swap(gs, "core"))

    chunks = []
    for group in GROUPS:
        xc = jnp.concatenate([shards[d][i] for d in group for i in (0, 2)])
        gc = jnp.concatenate([shards[d][i] for d in group for i in (1, 3)])
        rows = xc.shape[0] // ngy
        sums = jnp.concatenate([dot(xc, w1, 1, 0).astype(BF), dot(gc, w2, 1, 1).astype(BF)], axis=1)
        got = lax.all_to_all(sums.reshape(ngy, rows, 2 * ff), GY, 0, 0)
        total = jnp.sum(got.astype(F32), axis=0)
        hid, gp = gelu_local(total[:, :ff], total[:, ff:])
        act = jnp.concatenate([hid, gp], axis=1)
        acts = lax.all_to_all(jnp.broadcast_to(act[None], (ngy, rows, 2 * ff)), GY, 0, 0)
        acts = acts.reshape(ngy * rows, 2 * ff)
        chunks.append((group, xc, gc, acts[:, :ff], acts[:, ff:]))

    own = None
    for group, xc, gc, hid, gp in chunks:
        back = dot(gp, w1, 1, 1)
        for n, d in enumerate(group):
            mine = back[2 * n * half : (2 * n + 1) * half]
            other = back[(2 * n + 1) * half : (2 * n + 2) * half]
            both = mine + swap(other.astype(BF), "core").astype(F32)
            if d:
                both = shift(both.astype(BF), "z", nz, -d).astype(F32)
            own = both if own is None else own + both
    own = own + swap(own.astype(BF), "yhi").astype(F32)
    own = own.astype(BF)
    theirs = swap(own, "core")
    first = core == 0
    grad_inputs = jnp.concatenate([jnp.where(first, own, theirs), jnp.where(first, theirs, own)])

    x_all = jnp.concatenate([c[1] for c in chunks])
    g_all = jnp.concatenate([c[2] for c in chunks])
    hid_all = jnp.concatenate([c[3] for c in chunks])
    gp_all = jnp.concatenate([c[4] for c in chunks])
    grad_w_second = dot(hid_all, g_all, 0, 0).astype(BF)
    grad_w_first = dot(x_all, gp_all, 0, 0).astype(BF)
    return (grad_inputs, grad_w_first, grad_w_second)


def solution(mesh):
    devices = mesh.devices.reshape(mesh.devices.shape[0], 2, -1, 2, 2)
    fine = Mesh(devices, ("z", "ylo", "x", "yhi", "core"))
    units = ("z", "yhi", "core")
    in_specs = (P("z", GY), P(GY, units), P(units, GY), P("z", GY))
    out_specs = (P("z", GY), P(GY, units), P(units, GY))
    return jax.shard_map(
        on_device, mesh=fine, in_specs=in_specs, out_specs=out_specs, check_vma=False
    )
```

```python
import functools
import math

import jax
import jax.numpy as jnp
from jax import lax
from jax.experimental import pallas as pl
from jax.experimental.pallas import tpu as pltpu
from jax.sharding import Mesh, PartitionSpec as P

root_coef = math.sqrt(2.0 / math.pi)
cubic_coef = 0.044715
BF = jnp.bfloat16
F32 = jnp.float32
GY = ("ylo", "x")
NX = 4
GROUPS = ((1, -1, 2, -2), (3, -3), (4, 0))
VMEM = pl.BlockSpec(memory_space=pltpu.VMEM)
SMEM = pl.BlockSpec(memory_space=pltpu.SMEM)


def gelu_pair(pre):
    inner = root_coef * (pre + cubic_coef * pre * pre * pre)
    tanh_val = jnp.tanh(inner)
    value = 0.5 * pre * (1.0 + tanh_val)
    slope = 0.5 * (1.0 + tanh_val) + 0.5 * pre * (1.0 - tanh_val * tanh_val) * root_coef * (
        1.0 + 3.0 * cubic_coef * pre * pre
    )
    return value, slope


def dot(a, b, ca, cb):
    return lax.dot_general(a, b, (((ca,), (cb,)), ((), ())), preferred_element_type=F32)


def shift(a, axis, size, by):
    return lax.ppermute(a, axis, [(i, (i + by) % size) for i in range(size)])


def swap(a, axis):
    return lax.ppermute(a, axis, [(0, 1), (1, 0)])


def shape(*dims, dtype=BF):
    return jax.ShapeDtypeStruct(dims, dtype)


def call(body, name, out_shape, in_specs, out_specs=None, grid=(), scratch=(), limit=40):
    if out_specs is None:
        out_specs = jax.tree.map(lambda _: VMEM, out_shape)
    return pl.pallas_call(
        body,
        name=name,
        out_shape=out_shape,
        grid=grid,
        in_specs=in_specs,
        out_specs=out_specs,
        scratch_shapes=scratch,
        compiler_params=pltpu.CompilerParams(vmem_limit_bytes=limit << 20),
    )


def pack_kernel(idx, x, g, out):
    rows = pl.ds(pl.multiple_of(idx[0] * 64, 64), 64)
    out[0] = x[rows, :]
    out[1] = g[rows, :]


def forward_kernel(n, idx, *refs):
    parts, (w1, w1o, w2, w2o), (s0, s1, s2, s3, xg), (full,) = (
        refs[: 2 * n],
        refs[2 * n : 2 * n + 4],
        refs[2 * n + 4 : 2 * n + 9],
        refs[2 * n + 9 :],
    )
    j = pl.program_id(0)
    width = parts[0].shape[-1]
    half = 64

    @pl.when(j == 0)
    def _():
        for i in range(n):
            rows = slice(i * half, (i + 1) * half)
            xg[rows, :width] = parts[2 * i][...].reshape(half, width)
            xg[rows, width:] = parts[2 * i + 1][...].reshape(half, width)

    x = xg[:, :width]
    g = xg[:, width:]
    block = w1.shape[1]
    units = 3 * block
    for k, value in enumerate(
        (dot(x, w1[...], 1, 0), dot(g, w2[...], 1, 1), dot(x, w1o[...], 1, 0), dot(g, w2o[...], 1, 1))
    ):
        full[:, pl.ds(pl.multiple_of(k * units + j * block, block), block)] = value.astype(BF)

    @pl.when(j == pl.num_programs(0) - 1)
    def _():
        quarter = full.shape[0] // NX
        for k, out in enumerate((s0, s1, s2, s3)):
            start = lax.rem(idx[1] + k, NX) * quarter
            out[...] = full[pl.ds(pl.multiple_of(start, quarter), quarter), :]


def forward(idx, shards, w1, w1o, w2, w2o):
    n = len(shards)
    rows, width, units = 64 * n, w1.shape[0], w1.shape[1]
    steps, block = 3, units // 3
    operands, specs = [], []
    for sx, sg in shards:
        for a, which in ((sx, 0), (sg, 1)):
            operands.append(a)
            if a.ndim == 3:
                specs.append(pl.BlockSpec((1, 64, width), lambda j, which=which: (which, 0, 0)))
            else:
                specs.append(pl.BlockSpec((64, width), lambda j: (0, 0)))
    col = pl.BlockSpec((width, block), lambda j: (0, j))
    row = pl.BlockSpec((block, width), lambda j: (j, 0))
    quarter = shape(rows // NX, 4 * units)
    outs = (quarter, quarter, quarter, quarter, shape(rows, 2 * width))
    return call(
        functools.partial(forward_kernel, n),
        "forward_sums",
        outs,
        [SMEM, *specs, col, col, row, row],
        tuple(pl.BlockSpec(o.shape, lambda j: (0, 0)) for o in outs),
        grid=(steps,),
        scratch=[pltpu.VMEM((rows, 4 * units), BF)],
    )(idx, *operands, w1, w1o, w2, w2o)


def sum_kernel(idx, a, b, c, d, keep, send):
    rows = keep.shape[0]
    for out, which in ((keep, idx[2]), (send, 1 - idx[2])):
        at = pl.ds(pl.multiple_of(which * rows, rows), rows)
        out[...] = (
            a[at, :].astype(F32) + b[at, :].astype(F32) + c[at, :].astype(F32) + d[at, :].astype(F32)
        ).astype(out.dtype)


def sum_over_x(idx, pieces):
    rows, width = pieces[0].shape
    half = shape(rows // 2, width, dtype=F32)
    return call(sum_kernel, "sum_over_x", (half, half), [SMEM] + [VMEM] * 4)(idx, *pieces)


def gelu_kernel(keep, got, out):
    units = keep.shape[1] // 4
    for k in (0, 2):
        at, after = slice(k * units, (k + 1) * units), slice((k + 1) * units, (k + 2) * units)
        value, slope = gelu_pair(keep[:, at] + got[:, at])
        out[:, at] = value.astype(BF)
        out[:, after] = ((keep[:, after] + got[:, after]) * slope).astype(BF)


def gelu_rows(keep, got):
    return call(gelu_kernel, "gelu_rows", shape(*keep.shape), [VMEM] * 2)(keep, got)


def stack_kernel(a, b, c, d, out):
    for k, ref in enumerate((a, b, c, d)):
        out[k] = ref[...]


def stack(pieces):
    return call(stack_kernel, "stack_x", shape(4, *pieces[0].shape), [VMEM] * 4)(*pieces)


def backward_kernel(group, idx, mine, theirs, w1, w1o, own, other, *outs):
    j = pl.program_id(0)
    eighth, units = mine.shape[1], w1.shape[1]

    @pl.when(j == 0)
    def _():
        for k in range(NX):
            at = lax.rem(idx[1] + NX - k, NX) * 2
            for ref, which in ((mine, idx[2]), (theirs, 1 - idx[2])):
                rows = pl.ds(pl.multiple_of((at + which) * eighth, eighth), eighth)
                own[rows, :] = ref[k, :, : 2 * units]
                other[rows, :] = ref[k, :, 2 * units :]

    value = dot(own[:, units:], w1[...], 1, 1) + dot(other[:, units:], w1o[...], 1, 1)
    for i, out in enumerate(outs):
        out[...] = value[i * 64 : (i + 1) * 64].astype(out.dtype)


def backward(idx, group, mine, theirs, w1, w1o):
    rows, width, units = 8 * mine.shape[1], w1.shape[0], w1.shape[1]
    steps = 3
    act = shape(rows, 2 * units)
    whole = pl.BlockSpec(mine.shape, lambda j: (0, 0, 0))
    weight = pl.BlockSpec((width // steps, units), lambda j: (j, 0))
    outs = [shape(64, width, dtype=BF if d else F32) for d in group]
    return call(
        functools.partial(backward_kernel, group),
        "backward_rows",
        (act, act, *outs),
        [SMEM, whole, whole, weight, weight],
        (
            pl.BlockSpec(act.shape, lambda j: (0, 0)),
            pl.BlockSpec(act.shape, lambda j: (0, 0)),
            *[pl.BlockSpec((64, width // steps), lambda j: (0, j)) for _ in outs],
        ),
        grid=(steps,),
    )(idx, mine, theirs, w1, w1o)


def add_kernel(*refs):
    total = refs[0][...]
    for ref in refs[1:-1]:
        total = total + ref[...].astype(F32)
    refs[-1][...] = total.astype(refs[-1].dtype)


def add(pieces, dtype):
    return call(add_kernel, "add_rows", shape(*pieces[0].shape, dtype=dtype), [VMEM] * len(pieces))(*pieces)


def place_kernel(idx, own, theirs, out):
    out[pl.ds(pl.multiple_of(idx[0] * 64, 64), 64), :] = own[...]
    out[pl.ds(pl.multiple_of((1 - idx[0]) * 64, 64), 64), :] = theirs[...]


def weight_kernel(n, *refs):
    total = None
    for a, b in zip(refs[:n], refs[n : 2 * n]):
        value = dot(a[...], b[...], 0, 0)
        total = value if total is None else total + value
    refs[-1][...] = total.astype(refs[-1].dtype)


def weight_grad(name, lhs, lhs_at, lhs_width, rhs, rhs_at, rhs_width, steps):
    n = len(lhs)
    block = lhs_width // steps
    return call(
        functools.partial(weight_kernel, n),
        name,
        shape(lhs_width, rhs_width),
        [pl.BlockSpec((a.shape[0], block), lambda j: (0, lhs_at // block + j)) for a in lhs]
        + [pl.BlockSpec((b.shape[0], rhs_width), lambda j: (0, rhs_at // rhs_width)) for b in rhs],
        pl.BlockSpec((block, rhs_width), lambda j: (j, 0)),
        grid=(steps,),
    )(*lhs, *rhs)


def after(value, *others):
    return lax.optimization_barrier((value, *others))[0]


def on_device(x, w1, w2, g):
    nz = lax.axis_size("z")
    width, units = w1.shape
    idx = jnp.stack([lax.axis_index(a) for a in ("core", "x", "ylo")]).astype(jnp.int32)

    pack = call(pack_kernel, "pack_rows", shape(2, 64, width), [SMEM, VMEM, VMEM])(idx, x, g)
    shards = {0: (pack, pack)}
    up = down = pack
    for k in range(1, nz // 2):
        up, down = shift(up, "z", nz, 1), shift(down, "z", nz, -1)
        shards[k], shards[-k] = (up, up), (down, down)
    shards[nz // 2] = (shift(up[0], "z", nz, 1), shift(down[1], "z", nz, -1))
    w1o, w2o = swap(w1, "core"), swap(w2, "core")

    xg, acts, sends = [], [], []
    for group in GROUPS:
        *slots, rows = forward(idx, [shards[d] for d in group], w1, w1o, w2, w2o)
        xg += [rows, swap(rows, "core")]
        pieces = slots[:1] + [shift(slots[k], "x", NX, k) for k in range(1, NX)]
        keep, send = sum_over_x(idx, pieces)
        act = gelu_rows(keep, swap(send, "ylo"))
        mine = stack([act] + [shift(act, "x", NX, k) for k in range(1, NX)])
        own, other, *outs = backward(idx, group, mine, swap(mine, "ylo"), w1, w1o)
        acts += [own, swap(other, "core")]
        for d, out in zip(group, outs):
            if d:
                sends.append(shift(out, "z", nz, -d))
            else:
                sends.insert(0, out)

    total = add(sends, F32)
    half = add([total, swap(total, "yhi")], BF)
    grad_inputs = call(place_kernel, "place_rows", shape(*x.shape), [SMEM, VMEM, VMEM])(
        idx, half, swap(half, "core")
    )
    grad_w_second = weight_grad("grad_w_second", acts, 0, units, xg, width, width, 3)
    grad_w_first = weight_grad("grad_w_first", xg, 0, width, acts, units, units, 6)
    return (grad_inputs, grad_w_first, grad_w_second)


def solution(mesh):
    devices = mesh.devices.reshape(mesh.devices.shape[0], 2, NX, 2, 2)
    fine = Mesh(devices, ("z", "ylo", "x", "yhi", "core"))
    hidden = ("z", "yhi", "core")
    in_specs = (P("z", GY), P(GY, hidden), P(hidden, GY), P("z", GY))
    out_specs = (P("z", GY), P(GY, hidden), P(hidden, GY))
    return jax.shard_map(
        on_device, mesh=fine, in_specs=in_specs, out_specs=out_specs, check_vma=False
    )
```

```python
import functools
import math

import jax
import jax.numpy as jnp
from jax import lax
from jax.experimental import pallas as pl
from jax.experimental.pallas import tpu as pltpu
from jax.sharding import Mesh, PartitionSpec as P

root_coef = math.sqrt(2.0 / math.pi)
cubic_coef = 0.044715
BF = jnp.bfloat16
F32 = jnp.float32
GY = ("ylo", "x")
NX = 4
GROUPS = ((1, -1, 2, -2), (3, -3), (4, 0))
COST = {"part_w_second": 4, "part_w_first": 4, "grad_w_second": 4, "grad_w_first": 4}
VMEM = pl.BlockSpec(memory_space=pltpu.VMEM)
SMEM = pl.BlockSpec(memory_space=pltpu.SMEM)
HBM = pl.BlockSpec(memory_space=pl.ANY)


def gelu_pair(pre):
    inner = root_coef * (pre + cubic_coef * pre * pre * pre)
    tanh_val = jnp.tanh(inner)
    value = 0.5 * pre * (1.0 + tanh_val)
    slope = 0.5 * (1.0 + tanh_val) + 0.5 * pre * (1.0 - tanh_val * tanh_val) * root_coef * (
        1.0 + 3.0 * cubic_coef * pre * pre
    )
    return value, slope


def dot(a, b, ca, cb):
    return lax.dot_general(a, b, (((ca,), (cb,)), ((), ())), preferred_element_type=F32)


def shift(a, axis, size, by):
    return lax.ppermute(a, axis, [(i, (i + by) % size) for i in range(size)])


def swap(a, axis):
    return lax.ppermute(a, axis, [(0, 1), (1, 0)])


def shape(*dims, dtype=BF):
    return jax.ShapeDtypeStruct(dims, dtype)


def call(body, name, out_shape, in_specs, out_specs=None, grid=(), scratch=(), limit=40):
    if out_specs is None:
        out_specs = jax.tree.map(lambda _: VMEM, out_shape)
    return pl.pallas_call(
        body,
        name=name,
        out_shape=out_shape,
        grid=grid,
        in_specs=in_specs,
        out_specs=out_specs,
        scratch_shapes=scratch,
        compiler_params=pltpu.CompilerParams(vmem_limit_bytes=limit << 20),
        cost_estimate=pl.CostEstimate(flops=COST.get(name, 1) * 10**9, bytes_accessed=1, transcendentals=0),
    )


def pack_kernel(idx, x, g, out, sem):
    rows = pl.ds(pl.multiple_of(idx[0] * 64, 64), 64)
    copies = [pltpu.make_async_copy(a.at[rows, :], out.at[i], sem.at[i]) for i, a in enumerate((x, g))]
    for copy in copies:
        copy.start()
    for copy in copies:
        copy.wait()


def load_kernel(a, b, a_out, b_out, sem):
    copies = [pltpu.make_async_copy(a, a_out, sem.at[0]), pltpu.make_async_copy(b, b_out, sem.at[1])]
    for copy in copies:
        copy.start()
    for copy in copies:
        copy.wait()


def forward_kernel(n, idx, *refs):
    parts, (w1, w1o, w2, w2o), (s0, s1, s2, s3, xg), (full,) = (
        refs[: 2 * n],
        refs[2 * n : 2 * n + 4],
        refs[2 * n + 4 : 2 * n + 9],
        refs[2 * n + 9 :],
    )
    j = pl.program_id(0)
    width = parts[0].shape[-1]
    half = 64

    @pl.when(j == 0)
    def _():
        for i in range(n):
            rows = slice(i * half, (i + 1) * half)
            xg[rows, :width] = parts[2 * i][...].reshape(half, width)
            xg[rows, width:] = parts[2 * i + 1][...].reshape(half, width)

    x = xg[:, :width]
    g = xg[:, width:]
    block = w1.shape[1]
    units = 3 * block
    for k, value in enumerate(
        (dot(x, w1[...], 1, 0), dot(g, w2[...], 1, 1), dot(x, w1o[...], 1, 0), dot(g, w2o[...], 1, 1))
    ):
        full[:, pl.ds(pl.multiple_of(k * units + j * block, block), block)] = value.astype(BF)

    @pl.when(j == pl.num_programs(0) - 1)
    def _():
        quarter = full.shape[0] // NX
        for k, out in enumerate((s0, s1, s2, s3)):
            start = lax.rem(idx[1] + k, NX) * quarter
            out[...] = full[pl.ds(pl.multiple_of(start, quarter), quarter), :]


def forward(idx, shards, w1, w1o, w2, w2o):
    n = len(shards)
    rows, width, units = 64 * n, w1.shape[0], w1.shape[1]
    steps, block = 3, units // 3
    operands, specs = [], []
    for sx, sg in shards:
        for a, which in ((sx, 0), (sg, 1)):
            operands.append(a)
            if a.ndim == 3:
                specs.append(pl.BlockSpec((1, 64, width), lambda j, which=which: (which, 0, 0)))
            else:
                specs.append(pl.BlockSpec((64, width), lambda j: (0, 0)))
    col = pl.BlockSpec((width, block), lambda j: (0, j))
    row = pl.BlockSpec((block, width), lambda j: (j, 0))
    quarter = shape(rows // NX, 4 * units)
    outs = (quarter, quarter, quarter, quarter, shape(rows, 2 * width))
    return call(
        functools.partial(forward_kernel, n),
        "forward_sums",
        outs,
        [SMEM, *specs, col, col, row, row],
        tuple(pl.BlockSpec(o.shape, lambda j: (0, 0)) for o in outs),
        grid=(steps,),
        scratch=[pltpu.VMEM((rows, 4 * units), BF)],
    )(idx, *operands, w1, w1o, w2, w2o)


def sum_kernel(idx, a, b, c, d, keep, send):
    rows = keep.shape[0]
    for out, which in ((keep, idx[2]), (send, 1 - idx[2])):
        at = pl.ds(pl.multiple_of(which * rows, rows), rows)
        out[...] = (
            a[at, :].astype(F32) + b[at, :].astype(F32) + c[at, :].astype(F32) + d[at, :].astype(F32)
        ).astype(out.dtype)


def sum_over_x(idx, pieces):
    rows, width = pieces[0].shape
    half = shape(rows // 2, width, dtype=F32)
    return call(sum_kernel, "sum_over_x", (half, half), [SMEM] + [VMEM] * 4)(idx, *pieces)


def gelu_kernel(keep, got, out):
    units = keep.shape[1] // 4
    for k in (0, 2):
        at, after = slice(k * units, (k + 1) * units), slice((k + 1) * units, (k + 2) * units)
        value, slope = gelu_pair(keep[:, at] + got[:, at])
        out[:, at] = value.astype(BF)
        out[:, after] = ((keep[:, after] + got[:, after]) * slope).astype(BF)


def gelu_rows(keep, got):
    return call(gelu_kernel, "gelu_rows", shape(*keep.shape), [VMEM] * 2)(keep, got)


def stack_kernel(*refs):
    for k, ref in enumerate(refs[:-1]):
        refs[-1][k] = ref[...]


def stack(pieces):
    n = len(pieces)
    return call(stack_kernel, "stack_rows", shape(n, *pieces[0].shape), [VMEM] * n)(*pieces)


def backward_kernel(group, n, idx, *refs):
    parts, (w1, w1o, own, other), outs = refs[:n], refs[n : n + 4], refs[n + 4 :]
    eighth, units = parts[0].shape[1], w1.shape[1]

    @pl.when(pl.program_id(0) == 0)
    def _():
        for p, ref in enumerate(parts):
            for q in range(ref.shape[0]):
                y, x = (p, q) if n == 2 else (q, p)
                half = idx[2] if y == 0 else 1 - idx[2]
                at = lax.rem(idx[1] + NX - x, NX) * 2 + half
                rows = pl.ds(pl.multiple_of(at * eighth, eighth), eighth)
                own[rows, :] = ref[q, :, : 2 * units]
                other[rows, :] = ref[q, :, 2 * units :]

    value = dot(own[:, units:], w1[...], 1, 1) + dot(other[:, units:], w1o[...], 1, 1)
    for i, out in enumerate(outs):
        out[...] = value[i * 64 : (i + 1) * 64].astype(out.dtype)


def backward(idx, group, parts, w1, w1o):
    rows, width, units = 8 * parts[0].shape[1], w1.shape[0], w1.shape[1]
    steps = 3
    act = shape(rows, 2 * units)
    weight = pl.BlockSpec((width // steps, units), lambda j: (j, 0))
    outs = [shape(64, width, dtype=BF if d else F32) for d in group]
    return call(
        functools.partial(backward_kernel, group, len(parts)),
        "backward_rows",
        (act, act, *outs),
        [SMEM, *[pl.BlockSpec(p.shape, lambda j: (0, 0, 0)) for p in parts], weight, weight],
        (
            pl.BlockSpec(act.shape, lambda j: (0, 0)),
            pl.BlockSpec(act.shape, lambda j: (0, 0)),
            *[pl.BlockSpec((64, width // steps), lambda j: (0, j)) for _ in outs],
        ),
        grid=(steps,),
    )(idx, *parts, w1, w1o)


def add_kernel(*refs):
    total = refs[0][...].astype(F32)
    for ref in refs[1:-1]:
        total = total + ref[...].astype(F32)
    refs[-1][...] = total.astype(refs[-1].dtype)


def add(pieces, dtype):
    return call(add_kernel, "add_rows", shape(*pieces[0].shape, dtype=dtype), [VMEM] * len(pieces))(*pieces)


def place_kernel(idx, own, theirs, out):
    out[pl.ds(pl.multiple_of(idx[0] * 64, 64), 64), :] = own[...]
    out[pl.ds(pl.multiple_of((1 - idx[0]) * 64, 64), 64), :] = theirs[...]


def weight_kernel(n, *refs):
    total = None if len(refs) == 2 * n + 1 else refs[2 * n][...].astype(F32)
    for a, b in zip(refs[:n], refs[n : 2 * n]):
        value = dot(a[...], b[...], 0, 0)
        total = value if total is None else total + value
    refs[-1][...] = total.astype(refs[-1].dtype)


def weight_grad(name, lhs, lhs_at, lhs_width, rhs, rhs_at, rhs_width, steps, given=()):
    n = len(lhs)
    block = lhs_width // steps
    return call(
        functools.partial(weight_kernel, n),
        name,
        shape(lhs_width, rhs_width),
        [pl.BlockSpec((a.shape[0], block), lambda j: (0, lhs_at // block + j)) for a in lhs]
        + [pl.BlockSpec((b.shape[0], rhs_width), lambda j: (0, rhs_at // rhs_width)) for b in rhs]
        + [pl.BlockSpec((block, rhs_width), lambda j: (j, 0)) for _ in given],
        pl.BlockSpec((block, rhs_width), lambda j: (j, 0)),
        grid=(steps,),
    )(*lhs, *rhs, *given)


def on_device(x, w1, w2, g):
    nz = lax.axis_size("z")
    width, units = w1.shape
    idx = jnp.stack([lax.axis_index(a) for a in ("core", "x", "ylo")]).astype(jnp.int32)
    last = [idx]

    def step(function, *args):
        leaves, tree = jax.tree.flatten(args)
        arrays = [i for i, leaf in enumerate(leaves) if isinstance(leaf, jax.Array)]
        held = lax.optimization_barrier((*[leaves[i] for i in arrays], last[0]))
        for i, value in zip(arrays, held):
            leaves[i] = value
        result = function(*jax.tree.unflatten(tree, leaves))
        last[0] = jax.tree.leaves(result)[0]
        return result

    def turn(a, by):
        return shift(a, "z", nz, by)

    two = pltpu.SemaphoreType.DMA((2,))
    pack = call(pack_kernel, "pack_rows", shape(2, 64, width), [SMEM, HBM, HBM], scratch=[two])(idx, x, g)
    last[0] = pack
    shards = {0: (pack, pack)}
    load = call(load_kernel, "load_weights", (shape(*w1.shape), shape(*w2.shape)), [HBM, HBM], scratch=[two])
    w1v, w2v = step(load, w1, w2)
    w1o, w2o = swap(w1, "core"), swap(w2, "core")
    up = down = pack
    for k in range(1, nz // 2):
        up, down = turn(up, 1), turn(down, -1)
        if k == 1:
            up, down, _ = lax.optimization_barrier((up, down, w1v))
        shards[k], shards[-k] = (up, up), (down, down)
    shards[nz // 2] = (turn(up[0], 1), turn(down[1], -1))
    xg, own, other = [], [], []

    def reduce_x(i):
        *slots, rows = step(forward, idx, [shards[d] for d in GROUPS[i]], w1v, w1o, w2v, w2o)
        xg.append(rows)
        return slots[:1] + [shift(slots[k], "x", NX, k) for k in range(1, NX)]

    def reduce_y(pieces):
        keep, send = step(sum_over_x, idx, pieces)
        return keep, swap(send, "ylo")

    def along_x(act):
        return [act] + [shift(act, "x", NX, k) for k in range(1, NX)]

    def along_y(act):
        return [act, swap(act, "ylo")]

    def back(i, parts):
        a, b, *outs = step(backward, idx, GROUPS[i], parts, w1v, w1o)
        own.append(a)
        other.append(b)
        return [turn(out, -d) if d else out for d, out in zip(GROUPS[i], outs)]

    x0 = reduce_x(0)
    x1 = reduce_x(1)
    y0 = reduce_y(x0)
    x2 = reduce_x(2)
    a0 = along_x(step(gelu_rows, *y0))
    y1 = reduce_y(x1)
    b0 = along_y(step(stack, a0))
    a1 = along_y(step(gelu_rows, *y1))
    y2 = reduce_y(x2)
    b1 = along_x(step(stack, a1))
    a2 = along_y(step(gelu_rows, *y2))
    s0 = back(0, b0)
    b2 = along_x(step(stack, a2))
    s1 = back(1, b1)
    t0 = step(add, s0, F32)
    s2 = back(2, b2)
    t1 = step(add, [t0, *s1], F32)

    total = step(add, [t1, *s2], F32)
    total_theirs = swap(total, "yhi")
    give_second = step(weight_grad, "part_w_second", other, 0, units, xg, width, width, 3)
    got_second = swap(give_second, "core")
    give_first = step(weight_grad, "part_w_first", xg, 0, width, other, units, units, 6)
    got_first = swap(give_first, "core")
    half = step(add, [total, total_theirs], BF)
    half_theirs = swap(half, "core")
    grad_w_second = step(weight_grad, "grad_w_second", own, 0, units, xg, width, width, 3, [got_second])
    grad_w_first = step(weight_grad, "grad_w_first", xg, 0, width, own, units, units, 6, [got_first])
    place = call(place_kernel, "place_rows", shape(*x.shape), [SMEM, VMEM, VMEM])
    grad_inputs = step(place, idx, half, half_theirs)
    return (grad_inputs, grad_w_first, grad_w_second)


def solution(mesh):
    devices = mesh.devices.reshape(mesh.devices.shape[0], 2, NX, 2, 2)
    fine = Mesh(devices, ("z", "ylo", "x", "yhi", "core"))
    hidden = ("z", "yhi", "core")
    in_specs = (P("z", GY), P(GY, hidden), P(hidden, GY), P("z", GY))
    out_specs = (P("z", GY), P(GY, hidden), P(hidden, GY))
    return jax.shard_map(
        on_device, mesh=fine, in_specs=in_specs, out_specs=out_specs, check_vma=False
    )
```

```python
import functools
import math

import jax
import jax.numpy as jnp
from jax import lax
from jax.experimental import pallas as pl
from jax.experimental.pallas import tpu as pltpu
from jax.sharding import Mesh, PartitionSpec as P

root_coef = math.sqrt(2.0 / math.pi)
cubic_coef = 0.044715
BF = jnp.bfloat16
F32 = jnp.float32
GY = ("ylo", "x")
NX = 4
HALF = 64
GROUPS = ((1, -1), (2, -2), (3, -3), (4, 0))
BY_X1, BY_X3, BY_Y = 0, 1, 2
REDUCE = ((BY_X1, BY_X3, BY_Y),) * 4
GATHER = ((BY_X1, BY_X3, BY_Y), (BY_Y, BY_X1, BY_X3), (BY_X1, BY_X3, BY_Y), (BY_X3, BY_Y, BY_X1))
ORDER = (
    ("F", 0), ("F", 1), ("R1", 0), ("F", 2), ("R2", 0), ("R1", 1), ("G", 0),
    ("F", 3), ("R2", 1), ("J1", 0), ("R1", 2), ("G", 1), ("J2", 0), ("R2", 2),
    ("J1", 1), ("R1", 3), ("G", 2), ("J2", 1), ("B", 0), ("R2", 3), ("J1", 2),
    ("G", 3), ("J2", 2), ("B", 1), ("J1", 3), ("J2", 3), ("B", 2), ("B", 3),
)
COST = {"part_w_second": 30, "part_w_first": 30, "grad_w_second": 30, "grad_w_first": 30}
VMEM = pl.BlockSpec(memory_space=pltpu.VMEM)
SMEM = pl.BlockSpec(memory_space=pltpu.SMEM)
HBM = pl.BlockSpec(memory_space=pltpu.HBM)


def gelu_pair(pre):
    inner = root_coef * (pre + cubic_coef * pre * pre * pre)
    tanh_val = jnp.tanh(inner)
    value = 0.5 * pre * (1.0 + tanh_val)
    slope = 0.5 * (1.0 + tanh_val) + 0.5 * pre * (1.0 - tanh_val * tanh_val) * root_coef * (
        1.0 + 3.0 * cubic_coef * pre * pre
    )
    return value, slope


def dot(a, b, ca, cb):
    return lax.dot_general(a, b, (((ca,), (cb,)), ((), ())), preferred_element_type=F32)


def shift(a, axis, size, by):
    return lax.ppermute(a, axis, [(i, (i + by) % size) for i in range(size)])


def swap(a, axis):
    return lax.ppermute(a, axis, [(0, 1), (1, 0)])


def shape(*dims, dtype=BF):
    return jax.ShapeDtypeStruct(dims, dtype)


def call(body, name, out_shape, in_specs, out_specs=None, grid=(), scratch=(), limit=40):
    if out_specs is None:
        out_specs = jax.tree.map(lambda _: VMEM, out_shape)
    return pl.pallas_call(
        body,
        name=name,
        out_shape=out_shape,
        grid=grid,
        in_specs=in_specs,
        out_specs=out_specs,
        scratch_shapes=scratch,
        compiler_params=pltpu.CompilerParams(vmem_limit_bytes=limit << 20),
        cost_estimate=pl.CostEstimate(flops=COST.get(name, 1) * 10**9, bytes_accessed=1, transcendentals=0),
    )


def pack_kernel(idx, x, g, out, sem):
    rows = pl.ds(pl.multiple_of(idx[0] * 64, 64), 64)
    copies = [pltpu.make_async_copy(a.at[rows, :], out.at[i], sem.at[i]) for i, a in enumerate((x, g))]
    for copy in copies:
        copy.start()
    for copy in copies:
        copy.wait()


def load_kernel(a, b, a_out, b_out, sem):
    copies = [pltpu.make_async_copy(a, a_out, sem.at[0]), pltpu.make_async_copy(b, b_out, sem.at[1])]
    for copy in copies:
        copy.start()
    for copy in copies:
        copy.wait()


def neighbour(a, which):
    if which == BY_Y:
        return swap(a, "ylo")
    mask = 1 if which == BY_X1 else 3
    return lax.ppermute(a, "x", [(i, i ^ mask) for i in range(NX)])


def block_start(idx, flags, rows):
    x = idx[1]
    if flags[BY_X1]:
        x = jnp.bitwise_xor(x, 1)
    if flags[BY_X3]:
        x = jnp.bitwise_xor(x, 3)
    y = 1 - idx[2] if flags[BY_Y] else idx[2]
    return pl.multiple_of((x * 2 + y) * rows, rows)


def flags_of(code, order):
    flags = [0, 0, 0]
    for bit, which in enumerate(order):
        flags[which] = (code >> (2 - bit)) & 1
    return flags


def forward_kernel(n, order, idx, *refs):
    parts, (w1, w1o, w2, w2o), (keep, send, xg), (full,) = (
        refs[: 2 * n],
        refs[2 * n : 2 * n + 4],
        refs[2 * n + 4 : 2 * n + 7],
        refs[2 * n + 7 :],
    )
    width, units = w1.shape
    for i in range(n):
        rows = slice(i * HALF, (i + 1) * HALF)
        for k in (0, 1):
            ref = parts[2 * i + k]
            xg[rows, k * width : (k + 1) * width] = ref[k] if len(ref.shape) == 3 else ref[...]
    x, g = xg[:, :width], xg[:, width:]
    block = 256
    for j in range(0, units, block):
        at = slice(j, j + block)
        for k, value in enumerate(
            (dot(x, w1[:, at], 1, 0), dot(g, w2[at, :], 1, 1), dot(x, w1o[:, at], 1, 0), dot(g, w2o[at, :], 1, 1))
        ):
            full[:, k * units + j : k * units + j + block] = value
    rows = keep.shape[1]
    for code in range(8):
        value = full[pl.ds(block_start(idx, flags_of(code, order), rows), rows), :]
        if code < 4:
            keep[code] = value
        else:
            send[code - 4] = value.astype(send.dtype)


def forward(idx, shards, order, w1, w1o, w2, w2o):
    n = len(shards)
    rows, width, units = HALF * n, w1.shape[0], w1.shape[1]
    half = (4, rows // 8, 4 * units)
    operands = [a for pair in shards for a in pair]
    outs = (shape(*half, dtype=F32), shape(*half), shape(rows, 2 * width))
    return call(
        functools.partial(forward_kernel, n, order),
        "forward_sums",
        outs,
        [SMEM] + [VMEM] * (2 * n + 4),
        scratch=[pltpu.VMEM((rows, 4 * units), F32)],
    )(idx, *operands, w1, w1o, w2, w2o)


def halve_kernel(kept, got, keep, send):
    n = keep.shape[0]
    keep[...] = kept[:n] + got[:n].astype(F32)
    send[...] = (kept[n:] + got[n:].astype(F32)).astype(send.dtype)


def halve(kept, got, dtype):
    half = (kept.shape[0] // 2, *kept.shape[1:])
    return call(halve_kernel, "halve_sums", (shape(*half, dtype=F32), shape(*half, dtype=dtype)), [VMEM] * 2)(kept, got)


def gelu_kernel(keep, got, out):
    units = keep.shape[2] // 4
    for k in (0, 2):
        at, after = slice(k * units, (k + 1) * units), slice((k + 1) * units, (k + 2) * units)
        value, slope = gelu_pair(keep[0, :, at] + got[0, :, at])
        out[0, :, at] = value.astype(BF)
        out[0, :, after] = ((keep[0, :, after] + got[0, :, after]) * slope).astype(BF)


def gelu_rows(keep, got):
    return call(gelu_kernel, "gelu_rows", shape(*keep.shape), [VMEM] * 2)(keep, got)


def join_kernel(a, b, out):
    n = a.shape[0]
    out[:n] = a[...]
    out[n:] = b[...]


def join(a, b):
    return call(join_kernel, "join_rows", shape(2 * a.shape[0], *a.shape[1:]), [VMEM] * 2)(a, b)


def backward_kernel(order, idx, mine, theirs, w1, w1o, own, other, *outs):
    eighth = mine.shape[1]
    width, units = w1.shape
    for code in range(8):
        rows = pl.ds(block_start(idx, flags_of(code, order[::-1]), eighth), eighth)
        ref = mine if code < 4 else theirs
        own[rows, :] = ref[code % 4, :, : 2 * units]
        other[rows, :] = ref[code % 4, :, 2 * units :]
    block = 512
    for j in range(0, width, block):
        at = slice(j, j + block)
        value = dot(own[:, units:], w1[at, :], 1, 1) + dot(other[:, units:], w1o[at, :], 1, 1)
        for i, out in enumerate(outs):
            out[:, at] = value[i * HALF : (i + 1) * HALF].astype(out.dtype)


def backward(idx, group, order, mine, theirs, w1, w1o):
    rows, width, units = 8 * mine.shape[1], w1.shape[0], w1.shape[1]
    act = shape(rows, 2 * units)
    outs = [shape(HALF, width, dtype=BF if d else F32) for d in group]
    return call(
        functools.partial(backward_kernel, order), "backward_rows", (act, act, *outs), [SMEM] + [VMEM] * 4
    )(idx, mine, theirs, w1, w1o)


def add_kernel(*refs):
    total = refs[0][...]
    for ref in refs[1:-2]:
        total = total + ref[...].astype(F32)
    refs[-2][...] = total
    refs[-1][...] = total.astype(BF)


def add(pieces, _):
    rows = pieces[0].shape
    return call(add_kernel, "add_rows", (shape(*rows, dtype=F32), shape(*rows)), [VMEM] * len(pieces))(*pieces)


def pair_kernel(a, b, out):
    out[...] = (a[...].astype(F32) + b[...].astype(F32)).astype(out.dtype)


def add_pair(a, b, dtype):
    return call(pair_kernel, "add_pair", shape(*a.shape, dtype=dtype), [VMEM] * 2)(a, b)


def place_kernel(idx, own, theirs, out):
    out[pl.ds(pl.multiple_of(idx[0] * 64, 64), 64), :] = own[...]
    out[pl.ds(pl.multiple_of((1 - idx[0]) * 64, 64), 64), :] = theirs[...]


def weight_kernel(n, *refs):
    total = None if len(refs) == 2 * n + 1 else refs[2 * n][...].astype(F32)
    for a, b in zip(refs[:n], refs[n : 2 * n]):
        value = dot(a[...], b[...], 0, 0)
        total = value if total is None else total + value
    refs[-1][...] = total.astype(refs[-1].dtype)


def weight_grad(name, lhs, lhs_at, lhs_width, rhs, rhs_at, rhs_width, steps, given=()):
    n = len(lhs)
    block = lhs_width // steps
    return call(
        functools.partial(weight_kernel, n),
        name,
        shape(lhs_width, rhs_width),
        [pl.BlockSpec((a.shape[0], block), lambda j: (0, lhs_at // block + j)) for a in lhs]
        + [pl.BlockSpec((b.shape[0], rhs_width), lambda j: (0, rhs_at // rhs_width)) for b in rhs]
        + [pl.BlockSpec((block, rhs_width), lambda j: (j, 0)) for _ in given],
        pl.BlockSpec((block, rhs_width), lambda j: (j, 0)),
        grid=(steps,),
    )(*lhs, *rhs, *given)


def on_device(x, w1, w2, g):
    nz = lax.axis_size("z")
    width, units = w1.shape
    idx = jnp.stack([lax.axis_index(a) for a in ("core", "x", "ylo")]).astype(jnp.int32)
    last = [idx]

    def step(function, *args):
        leaves, tree = jax.tree.flatten(args)
        arrays = [i for i, leaf in enumerate(leaves) if isinstance(leaf, jax.Array)]
        held = lax.optimization_barrier((*[leaves[i] for i in arrays], last[0]))
        for i, value in zip(arrays, held):
            leaves[i] = value
        result = function(*jax.tree.unflatten(tree, leaves))
        last[0] = jax.tree.leaves(result)[0]
        return result

    def turn(a, by):
        return shift(a, "z", nz, by)

    two = pltpu.SemaphoreType.DMA((2,))
    pack = call(pack_kernel, "pack_rows", shape(2, 64, width), [SMEM, HBM, HBM], scratch=[two])(idx, x, g)
    last[0] = pack
    shards = {0: (pack, pack)}
    load = call(load_kernel, "load_weights", (shape(*w1.shape), shape(*w2.shape)), [HBM, HBM], scratch=[two])
    w1v, w2v = step(load, w1, w2)
    w1o, w2o = swap(w1, "core"), swap(w2, "core")
    up = down = pack
    for k in range(1, nz // 2):
        up, down = turn(up, 1), turn(down, -1)
        if k == 1:
            up, down, _ = lax.optimization_barrier((up, down, w1v))
        shards[k], shards[-k] = (up, up), (down, down)
    up = turn(up, 1)
    shards[nz // 2] = (up, up)
    xg, own, other = ([None] * len(GROUPS) for _ in range(3))

    state = {}

    def run(name, i):
        order, back = REDUCE[i], GATHER[i]
        if name == "F":
            keep, send, rows = step(forward, idx, [shards[d] for d in GROUPS[i]], order, w1v, w1o, w2v, w2o)
            xg[i] = rows
            state[i] = keep, neighbour(send, order[0])
        elif name in ("R1", "R2"):
            keep, send = step(halve, *state[i], BF if name == "R1" else F32)
            state[i] = keep, neighbour(send, order[1 if name == "R1" else 2])
        elif name == "G":
            act = step(gelu_rows, *state[i])
            state[i] = act, neighbour(act, back[0])
        elif name in ("J1", "J2"):
            act = step(join, *state[i])
            state[i] = act, neighbour(act, back[1 if name == "J1" else 2])
        else:
            a, b, *outs = step(backward, idx, GROUPS[i], back, *state[i], w1v, w1o)
            own[i], other[i] = a, b
            state[i] = [turn(out, -d) if d else out for d, out in zip(GROUPS[i], outs)]

    for entry in ORDER:
        run(*entry)
        if entry == ("B", 1):
            near = step(add_pair, *state[0], F32)

    give_first = weight_grad("part_w_first", xg, 0, width, other, units, units, 6)
    got_first = swap(give_first, "core")
    near, _ = step(add, [near, *state[1]], give_first)
    give_second = weight_grad("part_w_second", other, 0, units, xg, width, width, 3)
    got_second = swap(give_second, "core")
    grad_w_first = weight_grad("grad_w_first", xg, 0, width, own, units, units, 6, [got_first])
    sends = [near] + state[2] + state[3]
    total, give = step(add, sends, grad_w_first)
    total_theirs = swap(give, "yhi")
    grad_w_second = weight_grad("grad_w_second", own, 0, units, xg, width, width, 3, [got_second])
    last[0] = grad_w_second
    half = step(add_pair, total, total_theirs, BF)
    half_theirs = swap(half, "core")
    place = call(place_kernel, "place_rows", shape(*x.shape), [SMEM, VMEM, VMEM])
    grad_inputs = step(place, idx, half, half_theirs)
    return (grad_inputs, grad_w_first, grad_w_second)


def solution(mesh):
    devices = mesh.devices.reshape(mesh.devices.shape[0], 2, NX, 2, 2)
    fine = Mesh(devices, ("z", "ylo", "x", "yhi", "core"))
    hidden = ("z", "yhi", "core")
    in_specs = (P("z", GY), P(GY, hidden), P(hidden, GY), P("z", GY))
    out_specs = (P("z", GY), P(GY, hidden), P(hidden, GY))
    return jax.shard_map(
        on_device, mesh=fine, in_specs=in_specs, out_specs=out_specs, check_vma=False
    )
```

```python
import functools
import math

import jax
import jax.numpy as jnp
from jax import lax
from jax.experimental import pallas as pl
from jax.experimental.pallas import tpu as pltpu
from jax.sharding import Mesh, PartitionSpec as P

root_coef = math.sqrt(2.0 / math.pi)
cubic_coef = 0.044715
BF = jnp.bfloat16
F32 = jnp.float32
GY = ("ylo", "x")
NX = 4
HALF = 64
GROUPS = ((1, -1), (2, -2), (3, -3), (4, 0))
BY_X1, BY_X3, BY_Y = 0, 1, 2
REDUCE = ((BY_X1, BY_X3, BY_Y),) * 4
GATHER = ((BY_X1, BY_X3, BY_Y), (BY_Y, BY_X1, BY_X3), (BY_X1, BY_X3, BY_Y), (BY_X3, BY_Y, BY_X1))
ORDER = (
    ("F", 0), ("F", 1), ("R1", 0), ("F", 2), ("R2", 0), ("R1", 1), ("G", 0),
    ("F", 3), ("R2", 1), ("J1", 0), ("R1", 2), ("G", 1), ("J2", 0), ("R2", 2),
    ("J1", 1), ("R1", 3), ("G", 2), ("J2", 1), ("B", 0), ("R2", 3), ("J1", 2),
    ("G", 3), ("J2", 2), ("B", 1), ("J1", 3), ("J2", 3), ("B", 2), ("B", 3),
)
COST = {"part_w_second": 30, "part_w_first": 30, "grad_w_second": 30, "grad_w_first": 30}
VMEM = pl.BlockSpec(memory_space=pltpu.VMEM)
SMEM = pl.BlockSpec(memory_space=pltpu.SMEM)
HBM = pl.BlockSpec(memory_space=pltpu.HBM)


def gelu_pair(pre):
    inner = root_coef * (pre + cubic_coef * pre * pre * pre)
    tanh_val = jnp.tanh(inner)
    value = 0.5 * pre * (1.0 + tanh_val)
    slope = 0.5 * (1.0 + tanh_val) + 0.5 * pre * (1.0 - tanh_val * tanh_val) * root_coef * (
        1.0 + 3.0 * cubic_coef * pre * pre
    )
    return value, slope


def dot(a, b, ca, cb):
    return lax.dot_general(a, b, (((ca,), (cb,)), ((), ())), preferred_element_type=F32)


def shift(a, axis, size, by):
    return lax.ppermute(a, axis, [(i, (i + by) % size) for i in range(size)])


def swap(a, axis):
    return lax.ppermute(a, axis, [(0, 1), (1, 0)])


def shape(*dims, dtype=BF):
    return jax.ShapeDtypeStruct(dims, dtype)


def call(body, name, out_shape, in_specs, out_specs=None, grid=(), scratch=(), limit=40):
    if out_specs is None:
        out_specs = jax.tree.map(lambda _: VMEM, out_shape)
    return pl.pallas_call(
        body,
        name=name,
        out_shape=out_shape,
        grid=grid,
        in_specs=in_specs,
        out_specs=out_specs,
        scratch_shapes=scratch,
        compiler_params=pltpu.CompilerParams(vmem_limit_bytes=limit << 20),
        cost_estimate=pl.CostEstimate(flops=COST.get(name, 1) * 10**9, bytes_accessed=1, transcendentals=0),
    )


def pack_kernel(idx, x, g, out, sem):
    rows = pl.ds(pl.multiple_of(idx[0] * 64, 64), 64)
    copies = [pltpu.make_async_copy(a.at[rows, :], out.at[i], sem.at[i]) for i, a in enumerate((x, g))]
    for copy in copies:
        copy.start()
    for copy in copies:
        copy.wait()


def load_kernel(a, b, a_out, b_out, sem):
    copies = [pltpu.make_async_copy(a, a_out, sem.at[0]), pltpu.make_async_copy(b, b_out, sem.at[1])]
    for copy in copies:
        copy.start()
    for copy in copies:
        copy.wait()


def neighbour(a, which):
    if which == BY_Y:
        return swap(a, "ylo")
    mask = 1 if which == BY_X1 else 3
    return lax.ppermute(a, "x", [(i, i ^ mask) for i in range(NX)])


def block_start(idx, flags, rows):
    x = idx[1]
    if flags[BY_X1]:
        x = jnp.bitwise_xor(x, 1)
    if flags[BY_X3]:
        x = jnp.bitwise_xor(x, 3)
    y = 1 - idx[2] if flags[BY_Y] else idx[2]
    return pl.multiple_of((x * 2 + y) * rows, rows)


def flags_of(code, order):
    flags = [0, 0, 0]
    for bit, which in enumerate(order):
        flags[which] = (code >> (2 - bit)) & 1
    return flags


def forward_kernel(n, order, idx, *refs):
    parts, (w1, w1o, w2, w2o), (keep, send, xg), (full,) = (
        refs[: 2 * n],
        refs[2 * n : 2 * n + 4],
        refs[2 * n + 4 : 2 * n + 7],
        refs[2 * n + 7 :],
    )
    width, units = w1.shape
    for i in range(n):
        rows = slice(i * HALF, (i + 1) * HALF)
        for k in (0, 1):
            ref = parts[2 * i + k]
            xg[rows, k * width : (k + 1) * width] = ref[k] if len(ref.shape) == 3 else ref[...]
    x, g = xg[:, :width], xg[:, width:]
    block = 256
    for j in range(0, units, block):
        at = slice(j, j + block)
        for k, value in enumerate(
            (dot(x, w1[:, at], 1, 0), dot(g, w2[at, :], 1, 1), dot(x, w1o[:, at], 1, 0), dot(g, w2o[at, :], 1, 1))
        ):
            full[:, k * units + j : k * units + j + block] = value
    rows = keep.shape[1]
    for code in range(8):
        value = full[pl.ds(block_start(idx, flags_of(code, order), rows), rows), :]
        if code < 4:
            keep[code] = value
        else:
            send[code - 4] = value.astype(send.dtype)


def forward(idx, shards, order, w1, w1o, w2, w2o):
    n = len(shards)
    rows, width, units = HALF * n, w1.shape[0], w1.shape[1]
    half = (4, rows // 8, 4 * units)
    operands = [a for pair in shards for a in pair]
    outs = (shape(*half, dtype=F32), shape(*half), shape(rows, 2 * width))
    return call(
        functools.partial(forward_kernel, n, order),
        "forward_sums",
        outs,
        [SMEM] + [VMEM] * (2 * n + 4),
        scratch=[pltpu.VMEM((rows, 4 * units), F32)],
    )(idx, *operands, w1, w1o, w2, w2o)


def halve_kernel(kept, got, keep, send):
    n = keep.shape[0]
    keep[...] = kept[:n] + got[:n].astype(F32)
    send[...] = (kept[n:] + got[n:].astype(F32)).astype(send.dtype)


def halve(kept, got, dtype):
    half = (kept.shape[0] // 2, *kept.shape[1:])
    return call(halve_kernel, "halve_sums", (shape(*half, dtype=F32), shape(*half, dtype=dtype)), [VMEM] * 2)(kept, got)


def gelu_kernel(keep, got, out):
    units = keep.shape[2] // 4
    for k in (0, 2):
        at, after = slice(k * units, (k + 1) * units), slice((k + 1) * units, (k + 2) * units)
        value, slope = gelu_pair(keep[0, :, at] + got[0, :, at])
        out[0, :, at] = value.astype(BF)
        out[0, :, after] = ((keep[0, :, after] + got[0, :, after]) * slope).astype(BF)


def gelu_rows(keep, got):
    return call(gelu_kernel, "gelu_rows", shape(*keep.shape), [VMEM] * 2)(keep, got)


def join_kernel(a, b, out):
    n = a.shape[0]
    out[:n] = a[...]
    out[n:] = b[...]


def join(a, b):
    return call(join_kernel, "join_rows", shape(2 * a.shape[0], *a.shape[1:]), [VMEM] * 2)(a, b)


def backward_kernel(order, idx, mine, theirs, w1, w1o, own, other, *outs):
    eighth = mine.shape[1]
    width, units = w1.shape
    for code in range(8):
        rows = pl.ds(block_start(idx, flags_of(code, order[::-1]), eighth), eighth)
        ref = mine if code < 4 else theirs
        own[rows, :] = ref[code % 4, :, : 2 * units]
        other[rows, :] = ref[code % 4, :, 2 * units :]
    block = 512
    for j in range(0, width, block):
        at = slice(j, j + block)
        value = dot(own[:, units:], w1[at, :], 1, 1) + dot(other[:, units:], w1o[at, :], 1, 1)
        for i, out in enumerate(outs):
            out[:, at] = value[i * HALF : (i + 1) * HALF].astype(out.dtype)


def backward(idx, group, order, mine, theirs, w1, w1o):
    rows, width, units = 8 * mine.shape[1], w1.shape[0], w1.shape[1]
    act = shape(rows, 2 * units)
    outs = [shape(HALF, width, dtype=BF if d else F32) for d in group]
    return call(
        functools.partial(backward_kernel, order), "backward_rows", (act, act, *outs), [SMEM] + [VMEM] * 4
    )(idx, mine, theirs, w1, w1o)


def add_kernel(*refs):
    total = refs[0][...]
    for ref in refs[1:-2]:
        total = total + ref[...].astype(F32)
    refs[-2][...] = total
    refs[-1][...] = total.astype(BF)


def add(pieces, _):
    rows = pieces[0].shape
    return call(add_kernel, "add_rows", (shape(*rows, dtype=F32), shape(*rows)), [VMEM] * len(pieces))(*pieces)


def pair_kernel(a, b, out):
    out[...] = (a[...].astype(F32) + b[...].astype(F32)).astype(out.dtype)


def add_pair(a, b, dtype):
    return call(pair_kernel, "add_pair", shape(*a.shape, dtype=dtype), [VMEM] * 2)(a, b)


def place_kernel(idx, own, theirs, out):
    out[pl.ds(pl.multiple_of(idx[0] * 64, 64), 64), :] = own[...]
    out[pl.ds(pl.multiple_of((1 - idx[0]) * 64, 64), 64), :] = theirs[...]


def weight_kernel(n, *refs):
    a, b = (jnp.concatenate([ref[...] for ref in part]) for part in (refs[:n], refs[n : 2 * n]))
    total = dot(a, b, 0, 0)
    if len(refs) > 2 * n + 1:
        total = total + refs[2 * n][...].astype(F32)
    refs[-1][...] = total.astype(refs[-1].dtype)


def weight_grad(name, lhs, lhs_at, lhs_width, rhs, rhs_at, rhs_width, steps, given=()):
    n = len(lhs)
    block = lhs_width // steps
    return call(
        functools.partial(weight_kernel, n),
        name,
        shape(lhs_width, rhs_width),
        [pl.BlockSpec((a.shape[0], block), lambda j: (0, lhs_at // block + j)) for a in lhs]
        + [pl.BlockSpec((b.shape[0], rhs_width), lambda j: (0, rhs_at // rhs_width)) for b in rhs]
        + [pl.BlockSpec((block, rhs_width), lambda j: (j, 0)) for _ in given],
        pl.BlockSpec((block, rhs_width), lambda j: (j, 0)),
        grid=(steps,),
    )(*lhs, *rhs, *given)


def on_device(x, w1, w2, g):
    nz = lax.axis_size("z")
    width, units = w1.shape
    idx = jnp.stack([lax.axis_index(a) for a in ("core", "x", "ylo")]).astype(jnp.int32)
    last = [idx]

    def step(function, *args):
        leaves, tree = jax.tree.flatten(args)
        arrays = [i for i, leaf in enumerate(leaves) if isinstance(leaf, jax.Array)]
        held = lax.optimization_barrier((*[leaves[i] for i in arrays], last[0]))
        for i, value in zip(arrays, held):
            leaves[i] = value
        result = function(*jax.tree.unflatten(tree, leaves))
        last[0] = jax.tree.leaves(result)[0]
        return result

    def turn(a, by):
        return shift(a, "z", nz, by)

    two = pltpu.SemaphoreType.DMA((2,))
    pack = call(pack_kernel, "pack_rows", shape(2, 64, width), [SMEM, HBM, HBM], scratch=[two])(idx, x, g)
    last[0] = pack
    shards = {0: (pack, pack)}
    load = call(load_kernel, "load_weights", (shape(*w1.shape), shape(*w2.shape)), [HBM, HBM], scratch=[two])
    w1v, w2v = step(load, w1, w2)
    w1o, w2o = swap(w1, "core"), swap(w2, "core")
    up = down = pack
    for k in range(1, nz // 2):
        up, down = turn(up, 1), turn(down, -1)
        if k == 1:
            up, down, _ = lax.optimization_barrier((up, down, w1v))
        shards[k], shards[-k] = (up, up), (down, down)
    up = turn(up, 1)
    shards[nz // 2] = (up, up)
    xg, own, other = ([None] * len(GROUPS) for _ in range(3))

    state = {}

    def run(name, i):
        order, back = REDUCE[i], GATHER[i]
        if name == "F":
            keep, send, rows = step(forward, idx, [shards[d] for d in GROUPS[i]], order, w1v, w1o, w2v, w2o)
            xg[i] = rows
            state[i] = keep, neighbour(send, order[0])
        elif name in ("R1", "R2"):
            keep, send = step(halve, *state[i], BF if name == "R1" else F32)
            state[i] = keep, neighbour(send, order[1 if name == "R1" else 2])
        elif name == "G":
            act = step(gelu_rows, *state[i])
            state[i] = act, neighbour(act, back[0])
        elif name in ("J1", "J2"):
            act = step(join, *state[i])
            state[i] = act, neighbour(act, back[1 if name == "J1" else 2])
        else:
            a, b, *outs = step(backward, idx, GROUPS[i], back, *state[i], w1v, w1o)
            own[i], other[i] = a, b
            state[i] = [turn(out, -d) if d else out for d, out in zip(GROUPS[i], outs)]

    for entry in ORDER:
        run(*entry)
        if entry == ("B", 1):
            near = step(add_pair, *state[0], F32)

    give_first = weight_grad("part_w_first", xg, 0, width, other, units, units, 6)
    got_first = swap(give_first, "core")
    near, _ = step(add, [near, *state[1]], give_first)
    give_second = weight_grad("part_w_second", other, 0, units, xg, width, width, 3)
    got_second = swap(give_second, "core")
    grad_w_first = weight_grad("grad_w_first", xg, 0, width, own, units, units, 6, [got_first])
    sends = [near] + state[2] + state[3]
    total, give = step(add, sends, grad_w_first)
    total_theirs = swap(give, "yhi")
    grad_w_second = weight_grad("grad_w_second", own, 0, units, xg, width, width, 3, [got_second])
    last[0] = grad_w_second
    half = step(add_pair, total, total_theirs, BF)
    half_theirs = swap(half, "core")
    place = call(place_kernel, "place_rows", shape(*x.shape), [SMEM, VMEM, VMEM])
    grad_inputs = step(place, idx, half, half_theirs)
    return (grad_inputs, grad_w_first, grad_w_second)


def solution(mesh):
    devices = mesh.devices.reshape(mesh.devices.shape[0], 2, NX, 2, 2)
    fine = Mesh(devices, ("z", "ylo", "x", "yhi", "core"))
    hidden = ("z", "yhi", "core")
    in_specs = (P("z", GY), P(GY, hidden), P(hidden, GY), P("z", GY))
    out_specs = (P("z", GY), P(GY, hidden), P(hidden, GY))
    return jax.shard_map(
        on_device, mesh=fine, in_specs=in_specs, out_specs=out_specs, check_vma=False
    )
```

```python
import functools
import math

import jax
import jax.numpy as jnp
from jax import lax
from jax.experimental import pallas as pl
from jax.experimental.pallas import tpu as pltpu
from jax.sharding import Mesh, PartitionSpec as P

root_coef = math.sqrt(2.0 / math.pi)
cubic_coef = 0.044715
BF = jnp.bfloat16
F32 = jnp.float32
GY = ("ylo", "x")
NX = 4
HALF = 64
GROUPS = ((1, -1), (2, -2), (3, -3), (4, 0))
BY_X1, BY_X3, BY_Y = 0, 1, 2
REDUCE = ((BY_X1, BY_X3, BY_Y),) * 4
GATHER = ((BY_X1, BY_X3, BY_Y), (BY_Y, BY_X3, BY_X1), (BY_X1, BY_X3, BY_Y), (BY_X3, BY_Y, BY_X1))
ORDER = (
    ("F", 0), ("F", 1), ("R1", 0), ("F", 2), ("R2", 0), ("R1", 1), ("G", 0),
    ("F", 3), ("R2", 1), ("J1", 0), ("R1", 2), ("G", 1), ("J2", 0), ("R2", 2),
    ("J1", 1), ("R1", 3), ("G", 2), ("J2", 1), ("B", 0), ("R2", 3), ("J1", 2),
    ("G", 3), ("J2", 2), ("B", 1), ("J1", 3), ("J2", 3), ("B", 2), ("B", 3),
)
COST = {"part_w_second": 30, "part_w_first": 30, "grad_w_second": 30, "grad_w_first": 30}
VMEM = pl.BlockSpec(memory_space=pltpu.VMEM)
SMEM = pl.BlockSpec(memory_space=pltpu.SMEM)
HBM = pl.BlockSpec(memory_space=pltpu.HBM)


def gelu_pair(pre):
    inner = root_coef * (pre + cubic_coef * pre * pre * pre)
    tanh_val = jnp.tanh(inner)
    value = 0.5 * pre * (1.0 + tanh_val)
    slope = 0.5 * (1.0 + tanh_val) + 0.5 * pre * (1.0 - tanh_val * tanh_val) * root_coef * (
        1.0 + 3.0 * cubic_coef * pre * pre
    )
    return value, slope


def dot(a, b, ca, cb):
    return lax.dot_general(a, b, (((ca,), (cb,)), ((), ())), preferred_element_type=F32)


def shift(a, axis, size, by):
    return lax.ppermute(a, axis, [(i, (i + by) % size) for i in range(size)])


def swap(a, axis):
    return lax.ppermute(a, axis, [(0, 1), (1, 0)])


def shape(*dims, dtype=BF):
    return jax.ShapeDtypeStruct(dims, dtype)


def call(body, name, out_shape, in_specs, out_specs=None, grid=(), scratch=(), limit=40):
    if out_specs is None:
        out_specs = jax.tree.map(lambda _: VMEM, out_shape)
    return pl.pallas_call(
        body,
        name=name,
        out_shape=out_shape,
        grid=grid,
        in_specs=in_specs,
        out_specs=out_specs,
        scratch_shapes=scratch,
        compiler_params=pltpu.CompilerParams(vmem_limit_bytes=limit << 20),
        cost_estimate=pl.CostEstimate(flops=COST.get(name, 1) * 10**9, bytes_accessed=1, transcendentals=0),
    )


def pack_kernel(idx, x, g, out, sem):
    rows = pl.ds(pl.multiple_of(idx[0] * 64, 64), 64)
    copies = [pltpu.make_async_copy(a.at[rows, :], out.at[i], sem.at[i]) for i, a in enumerate((x, g))]
    for copy in copies:
        copy.start()
    for copy in copies:
        copy.wait()


def load_kernel(a, b, a_out, b_out, sem):
    copies = [pltpu.make_async_copy(a, a_out, sem.at[0]), pltpu.make_async_copy(b, b_out, sem.at[1])]
    for copy in copies:
        copy.start()
    for copy in copies:
        copy.wait()


def neighbour(a, which):
    if which == BY_Y:
        return swap(a, "ylo")
    mask = 1 if which == BY_X1 else 3
    return lax.ppermute(a, "x", [(i, i ^ mask) for i in range(NX)])


def block_start(idx, flags, rows):
    x = idx[1]
    if flags[BY_X1]:
        x = jnp.bitwise_xor(x, 1)
    if flags[BY_X3]:
        x = jnp.bitwise_xor(x, 3)
    y = 1 - idx[2] if flags[BY_Y] else idx[2]
    return pl.multiple_of((x * 2 + y) * rows, rows)


def flags_of(code, order):
    flags = [0, 0, 0]
    for bit, which in enumerate(order):
        flags[which] = (code >> (2 - bit)) & 1
    return flags


def forward_kernel(n, order, idx, *refs):
    parts, (w1, w1o, w2, w2o), (keep, send, xg), (full,) = (
        refs[: 2 * n],
        refs[2 * n : 2 * n + 4],
        refs[2 * n + 4 : 2 * n + 7],
        refs[2 * n + 7 :],
    )
    width, units = w1.shape
    for i in range(n):
        rows = slice(i * HALF, (i + 1) * HALF)
        for k in (0, 1):
            ref = parts[2 * i + k]
            xg[rows, k * width : (k + 1) * width] = ref[k] if len(ref.shape) == 3 else ref[...]
    x, g = xg[:, :width], xg[:, width:]
    block = 256
    for j in range(0, units, block):
        at = slice(j, j + block)
        for k, value in enumerate(
            (dot(x, w1[:, at], 1, 0), dot(g, w2[at, :], 1, 1), dot(x, w1o[:, at], 1, 0), dot(g, w2o[at, :], 1, 1))
        ):
            full[:, k * units + j : k * units + j + block] = value
    rows = keep.shape[1]
    for code in range(8):
        value = full[pl.ds(block_start(idx, flags_of(code, order), rows), rows), :]
        if code < 4:
            keep[code] = value
        else:
            send[code - 4] = value.astype(send.dtype)


def forward(idx, shards, order, w1, w1o, w2, w2o):
    n = len(shards)
    rows, width, units = HALF * n, w1.shape[0], w1.shape[1]
    half = (4, rows // 8, 4 * units)
    operands = [a for pair in shards for a in pair]
    outs = (shape(*half, dtype=F32), shape(*half), shape(rows, 2 * width))
    return call(
        functools.partial(forward_kernel, n, order),
        "forward_sums",
        outs,
        [SMEM] + [VMEM] * (2 * n + 4),
        scratch=[pltpu.VMEM((rows, 4 * units), F32)],
    )(idx, *operands, w1, w1o, w2, w2o)


def halve_kernel(kept, got, keep, send):
    n = keep.shape[0]
    keep[...] = kept[:n] + got[:n].astype(F32)
    send[...] = (kept[n:] + got[n:].astype(F32)).astype(send.dtype)


def halve(kept, got, dtype):
    half = (kept.shape[0] // 2, *kept.shape[1:])
    return call(halve_kernel, "halve_sums", (shape(*half, dtype=F32), shape(*half, dtype=dtype)), [VMEM] * 2)(kept, got)


def gelu_kernel(keep, got, out):
    units = keep.shape[2] // 4
    for k in (0, 2):
        at, after = slice(k * units, (k + 1) * units), slice((k + 1) * units, (k + 2) * units)
        value, slope = gelu_pair(keep[0, :, at] + got[0, :, at])
        out[0, :, at] = value.astype(BF)
        out[0, :, after] = ((keep[0, :, after] + got[0, :, after]) * slope).astype(BF)


def gelu_rows(keep, got):
    return call(gelu_kernel, "gelu_rows", shape(*keep.shape), [VMEM] * 2)(keep, got)


def join_kernel(a, b, out):
    n = a.shape[0]
    out[:n] = a[...]
    out[n:] = b[...]


def join(a, b):
    return call(join_kernel, "join_rows", shape(2 * a.shape[0], *a.shape[1:]), [VMEM] * 2)(a, b)


def backward_kernel(order, idx, mine, theirs, w1, w1o, own, other, *outs):
    eighth = mine.shape[1]
    width, units = w1.shape
    for code in range(8):
        rows = pl.ds(block_start(idx, flags_of(code, order[::-1]), eighth), eighth)
        ref = mine if code < 4 else theirs
        own[rows, :] = ref[code % 4, :, : 2 * units]
        other[rows, :] = ref[code % 4, :, 2 * units :]
    block = 512
    for j in range(0, width, block):
        at = slice(j, j + block)
        value = dot(own[:, units:], w1[at, :], 1, 1) + dot(other[:, units:], w1o[at, :], 1, 1)
        for i, out in enumerate(outs):
            out[:, at] = value[i * HALF : (i + 1) * HALF].astype(out.dtype)


def backward(idx, group, order, mine, theirs, w1, w1o):
    rows, width, units = 8 * mine.shape[1], w1.shape[0], w1.shape[1]
    act = shape(rows, 2 * units)
    outs = [shape(HALF, width, dtype=BF if d else F32) for d in group]
    return call(
        functools.partial(backward_kernel, order), "backward_rows", (act, act, *outs), [SMEM] + [VMEM] * 4
    )(idx, mine, theirs, w1, w1o)


def add_kernel(*refs):
    total = refs[0][...]
    for ref in refs[1:-2]:
        total = total + ref[...].astype(F32)
    refs[-2][...] = total
    refs[-1][...] = total.astype(BF)


def add(pieces, _):
    rows = pieces[0].shape
    return call(add_kernel, "add_rows", (shape(*rows, dtype=F32), shape(*rows)), [VMEM] * len(pieces))(*pieces)


def pair_kernel(a, b, out):
    out[...] = (a[...].astype(F32) + b[...].astype(F32)).astype(out.dtype)


def add_pair(a, b, dtype):
    return call(pair_kernel, "add_pair", shape(*a.shape, dtype=dtype), [VMEM] * 2)(a, b)


def place_kernel(idx, own, theirs, out):
    out[pl.ds(pl.multiple_of(idx[0] * 64, 64), 64), :] = own[...]
    out[pl.ds(pl.multiple_of((1 - idx[0]) * 64, 64), 64), :] = theirs[...]


def weight_kernel(n, *refs):
    a, b = (jnp.concatenate([ref[...] for ref in part]) for part in (refs[:n], refs[n : 2 * n]))
    total = dot(a, b, 0, 0)
    if len(refs) > 2 * n + 1:
        total = total + refs[2 * n][...].astype(F32)
    refs[-1][...] = total.astype(refs[-1].dtype)


def weight_grad(name, lhs, lhs_at, lhs_width, rhs, rhs_at, rhs_width, steps, given=()):
    n = len(lhs)
    block = lhs_width // steps
    return call(
        functools.partial(weight_kernel, n),
        name,
        shape(lhs_width, rhs_width),
        [pl.BlockSpec((a.shape[0], block), lambda j: (0, lhs_at // block + j)) for a in lhs]
        + [pl.BlockSpec((b.shape[0], rhs_width), lambda j: (0, rhs_at // rhs_width)) for b in rhs]
        + [pl.BlockSpec((block, rhs_width), lambda j: (j, 0)) for _ in given],
        pl.BlockSpec((block, rhs_width), lambda j: (j, 0)),
        grid=(steps,),
    )(*lhs, *rhs, *given)


def on_device(x, w1, w2, g):
    nz = lax.axis_size("z")
    width, units = w1.shape
    idx = jnp.stack([lax.axis_index(a) for a in ("core", "x", "ylo")]).astype(jnp.int32)
    last = [idx]

    def step(function, *args):
        leaves, tree = jax.tree.flatten(args)
        arrays = [i for i, leaf in enumerate(leaves) if isinstance(leaf, jax.Array)]
        held = lax.optimization_barrier((*[leaves[i] for i in arrays], last[0]))
        for i, value in zip(arrays, held):
            leaves[i] = value
        result = function(*jax.tree.unflatten(tree, leaves))
        last[0] = jax.tree.leaves(result)[0]
        return result

    def turn(a, by):
        return shift(a, "z", nz, by)

    two = pltpu.SemaphoreType.DMA((2,))
    pack = call(pack_kernel, "pack_rows", shape(2, 64, width), [SMEM, HBM, HBM], scratch=[two])(idx, x, g)
    last[0] = pack
    shards = {0: (pack, pack)}
    load = call(load_kernel, "load_weights", (shape(*w1.shape), shape(*w2.shape)), [HBM, HBM], scratch=[two])
    w1v, w2v = step(load, w1, w2)
    w1o, w2o = swap(w1, "core"), swap(w2, "core")
    up = down = pack
    for k in range(1, nz // 2):
        up, down = turn(up, 1), turn(down, -1)
        if k == 1:
            up, down, _ = lax.optimization_barrier((up, down, w1v))
        shards[k], shards[-k] = (up, up), (down, down)
    up = turn(up, 1)
    shards[nz // 2] = (up, up)
    xg, own, other = ([None] * len(GROUPS) for _ in range(3))

    state = {}

    def run(name, i):
        order, back = REDUCE[i], GATHER[i]
        if name == "F":
            keep, send, rows = step(forward, idx, [shards[d] for d in GROUPS[i]], order, w1v, w1o, w2v, w2o)
            xg[i] = rows
            state[i] = keep, neighbour(send, order[0])
        elif name in ("R1", "R2"):
            keep, send = step(halve, *state[i], BF if name == "R1" else F32)
            state[i] = keep, neighbour(send, order[1 if name == "R1" else 2])
        elif name == "G":
            act = step(gelu_rows, *state[i])
            state[i] = act, neighbour(act, back[0])
        elif name in ("J1", "J2"):
            act = step(join, *state[i])
            state[i] = act, neighbour(act, back[1 if name == "J1" else 2])
        else:
            a, b, *outs = step(backward, idx, GROUPS[i], back, *state[i], w1v, w1o)
            own[i], other[i] = a, b
            state[i] = [turn(out, -d) if d else out for d, out in zip(GROUPS[i], outs)]

    for entry in ORDER:
        run(*entry)
        if entry == ("B", 1):
            near = step(add_pair, *state[0], F32)

    give_first = weight_grad("part_w_first", xg, 0, width, other, units, units, 6)
    got_first = swap(give_first, "core")
    near, _ = step(add, [near, *state[1]], give_first)
    give_second = weight_grad("part_w_second", other, 0, units, xg, width, width, 3)
    got_second = swap(give_second, "core")
    grad_w_first = weight_grad("grad_w_first", xg, 0, width, own, units, units, 6, [got_first])
    sends = [near] + state[2] + state[3]
    total, give = step(add, sends, grad_w_first)
    total_theirs = swap(give, "yhi")
    grad_w_second = weight_grad("grad_w_second", own, 0, units, xg, width, width, 3, [got_second])
    last[0] = grad_w_second
    half = step(add_pair, total, total_theirs, BF)
    half_theirs = swap(half, "core")
    place = call(place_kernel, "place_rows", shape(*x.shape), [SMEM, VMEM, VMEM])
    grad_inputs = step(place, idx, half, half_theirs)
    return (grad_inputs, grad_w_first, grad_w_second)


def solution(mesh):
    devices = mesh.devices.reshape(mesh.devices.shape[0], 2, NX, 2, 2)
    fine = Mesh(devices, ("z", "ylo", "x", "yhi", "core"))
    hidden = ("z", "yhi", "core")
    in_specs = (P("z", GY), P(GY, hidden), P(hidden, GY), P("z", GY))
    out_specs = (P("z", GY), P(GY, hidden), P(hidden, GY))
    return jax.shard_map(
        on_device, mesh=fine, in_specs=in_specs, out_specs=out_specs, check_vma=False
    )
```
